32 devices in a mesh: space: 8 (over z, x), snap: 4 (over y, core).
Axes of the slice: x: 2, y: 2, z: 4, core: 2. Of those that a mesh axis runs over, the one named last changes fastest.
Arguments:
- velocity: bfloat16 [512, 3, 8, 8, 128], P('snap', None, 'space')
- metric: float32 [9, 8, 8, 128], P(None, 'space'), may hold values from -4 to 4
- volume: float32 [8, 8, 128], P('space'), may hold values from 3.6621095e-05 to 0.00036621094
- blade_mask: int32 [8, 8], P('space'), may hold values 0 or 1
Outputs:
- gram: float32 [512, 512], P('snap', 'space')
The draws below stay inside these ranges and needn't reach their ends.
All inputs are finite; a program needn't handle non-finite values. No bound on the sum of `blade_mask` on one device may be relied on, other than what follows from the above.
Results may differ from the reference program's by a relative error of at most 0.0003.
Values may be sent and summed in bfloat16 or wider, within the bound.
A program may use at most 64 MiB of HBM per device.

```python
import math
import jax
import jax.numpy as jnp
from jax import lax

SNAP_DEV = 128
CJ = 8
CK = 128
SNAPS = 512
NI = 8


def draw_velocity(key, part):
    key = jax.random.fold_in(key, 7)
    base_key, fluct_key = jax.random.split(key)
    base = jax.random.normal(base_key, (1, 3, NI, CJ, CK), jnp.float32)
    fluct = jax.random.normal(fluct_key, (SNAPS, 3, NI, CJ, CK), jnp.float32)
    return (base + 0.8 * fluct).astype(jnp.bfloat16)


def touch_ends(array, stream_key, least, largest):
    spot = [jax.random.randint(jax.random.fold_in(stream_key, axis), (), 0, length) for axis, length in enumerate(array.shape)]
    widest = array.shape.index(max(array.shape))
    beside = spot[:widest] + [(spot[widest] + 1) % array.shape[widest]] + spot[widest + 1:]
    return array.at[tuple(spot)].set(least).at[tuple(beside)].set(largest)


def steps_of(stream_key, extent, cuts, smallest, top_value):
    def one(dim, blocks):
        heights = jax.random.uniform(jax.random.fold_in(jax.random.fold_in(stream_key, 6), dim), (blocks,), jnp.float32, smallest / len(cuts), top_value / len(cuts))
        return jnp.repeat(jnp.exp(heights), extent[dim] // blocks).reshape((-1,) + (1,) * (len(extent) - dim - 1))

    gain = one(*cuts[0])
    for cut in cuts[1:]:
        gain = gain * one(*cut)
    return gain


def noise(rng, extent, width, most, cuts=(), kind=jnp.bfloat16):
    array = jax.random.normal(rng, extent, jnp.float32) * width
    if len(cuts) > 0:
        array = steps_of(rng, extent, cuts, -0.22, 0.18) * array
    return jnp.clip(array, min=-most, max=most).astype(kind)


def setup_inputs(seed: int = 0) -> dict:
    streams_of = jax.random.split(jax.random.key(seed), 5)
    velocity = draw_velocity(jax.random.fold_in(streams_of[4], 71), 0)
    metric = noise(streams_of[1], (9, NI, CJ, CK), 1.0, 4.0, ((1, 8),), jnp.float32)
    volume = jnp.clip(jnp.exp(math.log(0.00036621094) - 2.3025851 * jax.random.uniform(streams_of[2], (NI, CJ, CK), jnp.float32) ** steps_of(streams_of[2], (NI, CJ, CK), ((0, 8),), -0.2, 0.2)), 3.662109520519152e-05, 0.00036621094)
    blade_mask = touch_ends((jax.random.randint(streams_of[3], (NI, CJ), 0, 3) < 2).astype(jnp.int32), jax.random.fold_in(streams_of[3], 1), 0, 1)
    return {"velocity": velocity, "metric": metric, "volume": volume, "blade_mask": blade_mask}


def scaled_block(vel, metric, weight):
    field = vel.astype(jnp.float32)
    d_i = (jnp.roll(field, -1, axis=2) - jnp.roll(field, 1, axis=2)) * 0.5
    pad_j = jnp.pad(field, ((0, 0), (0, 0), (0, 0), (1, 1), (0, 0)))
    d_j = (pad_j[:, :, :, 2:, :] - pad_j[:, :, :, :-2, :]) * 0.5
    pad_k = jnp.pad(field, ((0, 0), (0, 0), (0, 0), (0, 0), (1, 1)))
    d_k = (pad_k[:, :, :, :, 2:] - pad_k[:, :, :, :, :-2]) * 0.5

    def deriv(comp, axis_a):
        return metric[3 * axis_a] * d_i[:, comp] + metric[3 * axis_a + 1] * d_j[:, comp] + metric[3 * axis_a + 2] * d_k[:, comp]
    omega_x = deriv(2, 1) - deriv(1, 2)
    omega_y = deriv(0, 2) - deriv(2, 0)
    omega_z = deriv(1, 0) - deriv(0, 1)
    vort = jnp.stack([omega_x, omega_y, omega_z], axis=1)
    return (vort * weight).astype(jnp.bfloat16)

def reference(velocity, metric, volume, blade_mask):
    weight = jnp.sqrt(volume * blade_mask.astype(jnp.float32)[:, :, None])
    blocks = velocity.reshape((SNAPS // SNAP_DEV, SNAP_DEV) + velocity.shape[1:])
    scaled = lax.map(lambda vel: scaled_block(vel, metric, weight), blocks)
    flat = scaled.reshape(SNAPS, -1).astype(jnp.float32)
    return jnp.dot(flat, flat.T, preferred_element_type=jnp.float32)
```

```python
import functools

import jax
import jax.numpy as jnp
from jax import lax
from jax.experimental import pallas as pl
from jax.experimental.pallas import tpu as pltpu
from jax.sharding import PartitionSpec as P

ROWS = 16


def remote(src, dst, send_sem, recv_sem, **where):
    return pltpu.make_async_remote_copy(
        src_ref=src,
        dst_ref=dst,
        send_sem=send_sem,
        recv_sem=recv_sem,
        device_id=where,
        device_id_type=pl.DeviceIdType.MESH,
    )


def kernel(
    n_space, n_snap, u_ref, coef_ref, out_ref,
    side, far, gathered, partial, landed,
    x_s, x_r, z_s, z_r, m_s, m_r, y_s, y_r, f_s, f_r, r_s, r_r,
):
    snaps, width = u_ref.shape
    cells = width // 3
    chunks = snaps // ROWS
    cols = landed.shape[1]
    per_dev = snaps // cols
    chips = n_snap // 2

    i = lax.axis_index("space")
    s = lax.axis_index("snap")
    odd = lax.rem(i, 2)
    core = lax.rem(s, 2)
    chip = s // 2
    partner = i + 1 - 2 * odd
    ahead = lax.rem(i + 2 - 4 * odd + n_space, n_space)
    mate = s + 1 - 2 * core

    def peer(o):
        return 2 * lax.rem(chip + o, chips) + core

    def origin(o):
        return 2 * lax.rem(chip + chips - o, chips) + core

    barrier = pltpu.get_barrier_semaphore()

    def greet(d, carry):
        pl.semaphore_signal(
            barrier, inc=1, device_id={"space": lax.rem(i + d, n_space)},
            device_id_type=pl.DeviceIdType.MESH,
        )
        return carry

    lax.fori_loop(1, n_space, greet, 0)
    pl.semaphore_signal(
        barrier, inc=1, device_id={"snap": mate}, device_id_type=pl.DeviceIdType.MESH
    )
    for o in range(1, chips):
        pl.semaphore_signal(
            barrier, inc=1, device_id={"snap": peer(o)}, device_id_type=pl.DeviceIdType.MESH
        )
    pl.semaphore_wait(barrier, n_space - 1 + chips)

    def rows(t):
        return pl.ds(pl.multiple_of(t * ROWS, ROWS), ROWS)

    def x_copy(t):
        return remote(u_ref.at[rows(t)], side.at[rows(t)], x_s.at[t], x_r.at[t], space=partner)

    def z_copy(t):
        return remote(side.at[rows(t)], far.at[rows(t)], z_s.at[t], z_r.at[t], space=ahead)

    def m_copy(t):
        block = gathered.at[s, rows(t)]
        return remote(block, block, m_s.at[t], m_r.at[t], snap=mate)

    def y_copy(o, t):
        block = gathered.at[s, rows(t)]
        return remote(block, block, y_s.at[o - 1, t], y_r.at[o - 1, t], snap=peer(o))

    def f_copy(o, t):
        block = gathered.at[origin(o), rows(t)]
        return remote(block, block, f_s.at[o - 1, t], f_r.at[o - 1, t], snap=mate)

    def y_arrival(o, t):
        block = gathered.at[origin(o), rows(t)]
        return remote(block, block, y_s.at[o - 1, t], y_r.at[o - 1, t], snap=peer(o))

    def m_arrival(t):
        block = gathered.at[mate, rows(t)]
        return remote(block, block, m_s.at[t], m_r.at[t], snap=mate)

    def f_origin(o):
        return 2 * lax.rem(chip + chips - o, chips) + 1 - core

    def f_arrival(o, t):
        block = gathered.at[f_origin(o), rows(t)]
        return remote(block, block, f_s.at[o - 1, t], f_r.at[o - 1, t], snap=mate)

    lane = lax.rem(lax.broadcasted_iota(jnp.int32, (ROWS, cells), 1), 128)
    sign = (1 - 2 * odd).astype(jnp.float32)

    def vorticity(t):
        d_i, d_j, d_k = [], [], []
        for c in range(3):
            part = pl.ds(c * cells, cells)
            here = u_ref[rows(t), part].astype(jnp.float32)
            near = side[rows(t), part].astype(jnp.float32)
            away = far[rows(t), part].astype(jnp.float32)
            d_i.append((near - away) * sign)
            edge = jnp.zeros((ROWS, 128), jnp.float32)
            d_j.append(
                jnp.concatenate([here[:, 128:], edge], axis=1)
                - jnp.concatenate([edge, here[:, :-128]], axis=1)
            )
            d_k.append(
                jnp.where(lane == 127, 0.0, pltpu.roll(here, cells - 1, 1))
                - jnp.where(lane == 0, 0.0, pltpu.roll(here, 1, 1))
            )

        def deriv(comp, a):
            return (
                coef_ref[pl.ds(3 * a, 1), :] * d_i[comp]
                + coef_ref[pl.ds(3 * a + 1, 1), :] * d_j[comp]
                + coef_ref[pl.ds(3 * a + 2, 1), :] * d_k[comp]
            )

        for c, (p, q) in enumerate(((2, 1), (0, 2), (1, 0))):
            gathered[s, rows(t), pl.ds(c * cells, cells)] = (
                deriv(p, q) - deriv(q, p)
            ).astype(jnp.bfloat16)

    def launch(t, carry):
        x_copy(t).start()
        return carry

    lax.fori_loop(0, chunks, launch, 0)

    def step(t, carry):
        @pl.when(t < chunks)
        def _():
            x_copy(t).wait_recv()
            z_copy(t).start()

        @pl.when(jnp.logical_and(t >= 1, t < chunks + 1))
        def _():
            z_copy(t - 1).wait_recv()
            vorticity(t - 1)
            for o in range(1, chips):
                y_copy(o, t - 1).start()
            m_copy(t - 1).start()

        @pl.when(t >= 3)
        def _():
            for o in range(1, chips):
                y_arrival(o, t - 3).wait_recv()
                f_copy(o, t - 3).start()

        return carry

    def r_copy(block):
        return remote(
            partial.at[block], landed.at[i], r_s.at[block], r_r.at[i], space=block
        )

    def r_arrival(source):
        return remote(
            partial.at[i], landed.at[source], r_s.at[source], r_r.at[source], space=source
        )

    def product(dev):
        own = gathered[s]
        for h in range(per_dev):
            block = dev * per_dev + h
            partial[block] = lax.dot_general(
                gathered[dev, pl.ds(h * cols, cols), :], own, (((1,), (1,)), ((), ())),
                preferred_element_type=jnp.float32,
            )

            @pl.when(block != i)
            def _():
                r_copy(block).start()

    lax.fori_loop(0, chunks + 1, step, 0)
    product(s)
    lax.fori_loop(chunks + 1, chunks + 3, step, 0)

    def await_m(t, carry):
        m_arrival(t).wait_recv()
        return carry

    lax.fori_loop(0, chunks, await_m, 0)
    product(mate)
    for o in range(1, chips):
        product(origin(o))
    for o in range(1, chips):
        def await_f(t, carry):
            f_arrival(o, t).wait_recv()
            return carry

        lax.fori_loop(0, chunks, await_f, 0)
        product(f_origin(o))

    def add(d, total):
        source = lax.rem(i + d, n_space)
        r_arrival(source).wait_recv()
        return total + landed[source]

    total = lax.fori_loop(1, n_space, add, partial[i])
    out_ref[...] = total

    def drain(t, carry):
        x_copy(t).wait_send()
        z_copy(t).wait_send()
        m_copy(t).wait_send()
        for o in range(1, chips):
            y_copy(o, t).wait_send()
            f_copy(o, t).wait_send()
        return carry

    lax.fori_loop(0, chunks, drain, 0)

    def drain_r(d, carry):
        r_copy(lax.rem(i + d, n_space)).wait_send()
        return carry

    lax.fori_loop(1, n_space, drain_r, 0)


def shards(n_space, n_snap, velocity, metric, volume, blade_mask):
    snaps = velocity.shape[0]
    u = velocity.reshape(snaps, -1)
    width = u.shape[1]
    weight = 0.5 * jnp.sqrt(volume * blade_mask.astype(jnp.float32)[:, :, None])
    coef = (metric * weight).reshape(9, -1)
    cols = snaps * n_snap // n_space
    chunks = snaps // ROWS
    chips = n_snap // 2
    far = max(chips - 1, 1)
    dma = pltpu.SemaphoreType.DMA
    return pl.pallas_call(
        functools.partial(kernel, n_space, n_snap),
        out_shape=jax.ShapeDtypeStruct((cols, snaps), jnp.float32),
        in_specs=[pl.BlockSpec(memory_space=pltpu.VMEM)] * 2,
        out_specs=pl.BlockSpec(memory_space=pltpu.VMEM),
        scratch_shapes=[
            pltpu.VMEM((snaps, width), jnp.bfloat16),
            pltpu.VMEM((snaps, width), jnp.bfloat16),
            pltpu.VMEM((n_snap, snaps, width), jnp.bfloat16),
            pltpu.VMEM((n_space, cols, snaps), jnp.float32),
            pltpu.VMEM((n_space, cols, snaps), jnp.float32),
            dma((chunks,)), dma((chunks,)), dma((chunks,)), dma((chunks,)),
            dma((chunks,)), dma((chunks,)),
            dma((far, chunks)), dma((far, chunks)), dma((far, chunks)), dma((far, chunks)),
            dma((n_space,)), dma((n_space,)),
        ],
        compiler_params=pltpu.CompilerParams(
            collective_id=0, has_side_effects=True, vmem_limit_bytes=48 * 1024 * 1024
        ),
    )(u, coef).T


def solution(mesh):
    in_specs = (
        P("snap", None, "space", None, None),
        P(None, "space", None, None),
        P("space", None, None),
        P("space", None),
    )
    body = functools.partial(shards, mesh.shape["space"], mesh.shape["snap"])
    return jax.shard_map(body, mesh=mesh, in_specs=in_specs, out_specs=P("snap", "space"), check_vma=False)
```

```python
import functools

import jax
import jax.numpy as jnp
from jax import lax
from jax.experimental import pallas as pl
from jax.experimental.pallas import tpu as pltpu
from jax.sharding import PartitionSpec as P

ROWS = 16


def remote(src, dst, send_sem, recv_sem, **where):
    return pltpu.make_async_remote_copy(
        src_ref=src,
        dst_ref=dst,
        send_sem=send_sem,
        recv_sem=recv_sem,
        device_id=where,
        device_id_type=pl.DeviceIdType.MESH,
    )


def kernel(
    n_space, n_snap, u_ref, metric_ref, volume_ref, mask_ref, out_ref,
    coef_ref, side, far, gathered, partial, landed,
    x_s, x_r, z_s, z_r, m_s, m_r, y_s, y_r, f_s, f_r, r_s, r_r,
):
    snaps, width = u_ref.shape
    cells = width // 3
    chunks = snaps // ROWS
    cols = landed.shape[1]
    per_dev = snaps // cols
    chips = n_snap // 2

    i = lax.axis_index("space")
    s = lax.axis_index("snap")
    odd = lax.rem(i, 2)
    core = lax.rem(s, 2)
    chip = s // 2
    partner = i + 1 - 2 * odd
    ahead = lax.rem(i + 2 - 4 * odd + n_space, n_space)
    mate = s + 1 - 2 * core

    def peer(o):
        return 2 * lax.rem(chip + o, chips) + core

    def origin(o):
        return 2 * lax.rem(chip + chips - o, chips) + core

    barrier = pltpu.get_barrier_semaphore()

    def greet(d, carry):
        pl.semaphore_signal(
            barrier, inc=1, device_id={"space": lax.rem(i + d, n_space)},
            device_id_type=pl.DeviceIdType.MESH,
        )
        return carry

    lax.fori_loop(1, n_space, greet, 0)
    pl.semaphore_signal(
        barrier, inc=1, device_id={"snap": mate}, device_id_type=pl.DeviceIdType.MESH
    )
    for o in range(1, chips):
        pl.semaphore_signal(
            barrier, inc=1, device_id={"snap": peer(o)}, device_id_type=pl.DeviceIdType.MESH
        )
    pl.semaphore_wait(barrier, n_space - 1 + chips)

    def rows(t):
        return pl.ds(pl.multiple_of(t * ROWS, ROWS), ROWS)

    def part(p):
        return pl.ds(p * cells, cells)

    def x_copy(t, p):
        where = (rows(t), part(p))
        return remote(u_ref.at[where], side.at[where], x_s.at[t, p], x_r.at[t, p], space=partner)

    def z_copy(t, p):
        block = (rows(t), part(p))
        return remote(side.at[block], far.at[block], z_s.at[t, p], z_r.at[t, p], space=ahead)

    def m_copy(t):
        block = gathered.at[s, rows(t)]
        return remote(block, block, m_s.at[t], m_r.at[t], snap=mate)

    def m_arrival(t):
        block = gathered.at[mate, rows(t)]
        return remote(block, block, m_s.at[t], m_r.at[t], snap=mate)

    def cross(source, o, t, p):
        block = gathered.at[source, rows(t), part(p)]
        return remote(block, block, y_s.at[o - 1, t, p], y_r.at[o - 1, t, p], snap=peer(o))

    def y_copy(o, t, p):
        return cross(s, o, t, p)

    def y_arrival(o, t, p):
        return cross(origin(o), o, t, p)

    def onward(source, o, t, p):
        block = gathered.at[source, rows(t), part(p)]
        return remote(block, block, f_s.at[o - 1, t, p], f_r.at[o - 1, t, p], snap=mate)

    def f_copy(o, t, p):
        return onward(origin(o), o, t, p)

    def f_origin(o):
        return 2 * lax.rem(chip + chips - o, chips) + 1 - core

    def f_arrival(o, t, p):
        return onward(f_origin(o), o, t, p)

    lane = lax.rem(lax.broadcasted_iota(jnp.int32, (ROWS, cells), 1), 128)
    sign = (1 - 2 * odd).astype(jnp.float32)

    def vorticity(t):
        d_i, d_j, d_k = [], [], []
        for c in range(3):
            here = u_ref[rows(t), part(c)].astype(jnp.float32)
            near = side[rows(t), part(c)].astype(jnp.float32)
            away = far[rows(t), part(c)].astype(jnp.float32)
            d_i.append((near - away) * sign)
            edge = jnp.zeros((ROWS, 128), jnp.float32)
            d_j.append(
                jnp.concatenate([here[:, 128:], edge], axis=1)
                - jnp.concatenate([edge, here[:, :-128]], axis=1)
            )
            d_k.append(
                jnp.where(lane == 127, 0.0, pltpu.roll(here, cells - 1, 1))
                - jnp.where(lane == 0, 0.0, pltpu.roll(here, 1, 1))
            )

        def deriv(comp, a):
            return (
                coef_ref[pl.ds(3 * a, 1), :] * d_i[comp]
                + coef_ref[pl.ds(3 * a + 1, 1), :] * d_j[comp]
                + coef_ref[pl.ds(3 * a + 2, 1), :] * d_k[comp]
            )

        for c, (p, q) in enumerate(((2, 1), (0, 2), (1, 0))):
            gathered[s, rows(t), part(c)] = (
                deriv(p, q) - deriv(q, p)
            ).astype(jnp.bfloat16)

    def launch(t, carry):
        for p in range(3):
            x_copy(t, p).start()
        return carry

    lax.fori_loop(0, chunks, launch, 0)

    for j in range(cells // 128):
        line = pl.ds(j, 1)
        weight = 0.5 * jnp.sqrt(volume_ref[line, :] * mask_ref[0, j].astype(jnp.float32))
        coef_ref[:, pl.ds(j * 128, 128)] = metric_ref[:, j, :] * weight

    def step(t, carry):
        @pl.when(t < chunks)
        def _():
            for p in range(3):
                x_copy(t, p).wait_recv()
                z_copy(t, p).start()

        @pl.when(jnp.logical_and(t >= 1, t < chunks + 1))
        def _():
            for p in range(3):
                z_copy(t - 1, p).wait_recv()
            vorticity(t - 1)
            for p in range(3):
                for o in range(1, chips):
                    y_copy(o, t - 1, p).start()
            m_copy(t - 1).start()

        @pl.when(t >= 3)
        def _():
            for p in range(3):
                for o in range(1, chips):
                    y_arrival(o, t - 3, p).wait_recv()
                    f_copy(o, t - 3, p).start()

        return carry

    def r_copy(block):
        return remote(
            partial.at[block], landed.at[i], r_s.at[block], r_r.at[i], space=block
        )

    def r_arrival(source):
        return remote(
            partial.at[i], landed.at[source], r_s.at[source], r_r.at[source], space=source
        )

    def product(dev, h):
        block = dev * per_dev + h
        partial[block] = lax.dot_general(
            gathered[dev, pl.ds(h * cols, cols), :], gathered[s], (((1,), (1,)), ((), ())),
            preferred_element_type=jnp.float32,
        )

        @pl.when(block != i)
        def _():
            r_copy(block).start()

    def await_m(t, carry):
        m_arrival(t).wait_recv()
        return carry

    per_block = cols // ROWS

    def product_f(o, h):
        def await_f(t, carry):
            for p in range(3):
                f_arrival(o, t, p).wait_recv()
            return carry

        lax.fori_loop(h * per_block, (h + 1) * per_block, await_f, 0)
        product(f_origin(o), h)

    lax.fori_loop(0, chunks + 1, step, 0)
    for h in range(per_dev):
        product(s, h)
    lax.fori_loop(0, chunks, await_m, 0)
    for h in range(per_dev):
        product(mate, h)
    lax.fori_loop(chunks + 1, chunks + 2, step, 0)
    for o in range(1, chips):
        for h in range(per_dev - 1):
            product(origin(o), h)
    lax.fori_loop(chunks + 2, chunks + 3, step, 0)
    for o in range(1, chips):
        for h in range(per_dev - 1):
            product_f(o, h)
    for o in range(1, chips):
        product(origin(o), per_dev - 1)
    for o in range(1, chips):
        product_f(o, per_dev - 1)

    def add(d, total):
        source = lax.rem(i + d, n_space)
        r_arrival(source).wait_recv()
        return total + landed[source]

    total = lax.fori_loop(1, n_space, add, partial[i])
    out_ref[...] = total

    def drain(t, carry):
        m_copy(t).wait_send()
        for p in range(3):
            x_copy(t, p).wait_send()
            z_copy(t, p).wait_send()
            for o in range(1, chips):
                y_copy(o, t, p).wait_send()
                f_copy(o, t, p).wait_send()
        return carry

    lax.fori_loop(0, chunks, drain, 0)

    def drain_r(d, carry):
        r_copy(lax.rem(i + d, n_space)).wait_send()
        return carry

    lax.fori_loop(1, n_space, drain_r, 0)


def shards(n_space, n_snap, velocity, metric, volume, blade_mask):
    snaps = velocity.shape[0]
    u = velocity.reshape(snaps, -1)
    width = u.shape[1]
    cols = snaps * n_snap // n_space
    chunks = snaps // ROWS
    chips = n_snap // 2
    far = max(chips - 1, 1)
    dma = pltpu.SemaphoreType.DMA
    return pl.pallas_call(
        functools.partial(kernel, n_space, n_snap),
        out_shape=jax.ShapeDtypeStruct((cols, snaps), jnp.float32),
        in_specs=[pl.BlockSpec(memory_space=pltpu.VMEM)] * 3
        + [pl.BlockSpec(memory_space=pltpu.SMEM)],
        out_specs=pl.BlockSpec(memory_space=pltpu.VMEM),
        scratch_shapes=[
            pltpu.VMEM((9, width // 3), jnp.float32),
            pltpu.VMEM((snaps, width), jnp.bfloat16),
            pltpu.VMEM((snaps, width), jnp.bfloat16),
            pltpu.VMEM((n_snap, snaps, width), jnp.bfloat16),
            pltpu.VMEM((n_space, cols, snaps), jnp.float32),
            pltpu.VMEM((n_space, cols, snaps), jnp.float32),
            dma((chunks, 3)), dma((chunks, 3)), dma((chunks, 3)), dma((chunks, 3)),
            dma((chunks,)), dma((chunks,)),
            dma((far, chunks, 3)), dma((far, chunks, 3)),
            dma((far, chunks, 3)), dma((far, chunks, 3)),
            dma((n_space,)), dma((n_space,)),
        ],
        compiler_params=pltpu.CompilerParams(
            collective_id=0, has_side_effects=True, vmem_limit_bytes=48 * 1024 * 1024
        ),
    )(u, metric[:, 0], volume[0], blade_mask).T


def solution(mesh):
    in_specs = (
        P("snap", None, "space", None, None),
        P(None, "space", None, None),
        P("space", None, None),
        P("space", None),
    )
    body = functools.partial(shards, mesh.shape["space"], mesh.shape["snap"])
    return jax.shard_map(body, mesh=mesh, in_specs=in_specs, out_specs=P("snap", "space"), check_vma=False)
```

```python
import functools

import jax
import jax.numpy as jnp
from jax import lax
from jax.experimental import pallas as pl
from jax.experimental.pallas import tpu as pltpu
from jax.sharding import PartitionSpec as P

ROWS = 16


def remote(src, dst, send_sem, recv_sem, **where):
    return pltpu.make_async_remote_copy(
        src_ref=src,
        dst_ref=dst,
        send_sem=send_sem,
        recv_sem=recv_sem,
        device_id=where,
        device_id_type=pl.DeviceIdType.MESH,
    )


def kernel(
    n_space, n_snap, u_ref, metric_ref, volume_ref, mask_ref, out_ref,
    coef_ref, side, far, gathered, partial, landed,
    x_s, x_r, z_s, z_r, m_s, m_r, y_s, y_r, f_s, f_r, r_s, r_r, ring, pair,
):
    snaps, width = u_ref.shape
    cells = width // 3
    chunks = snaps // ROWS
    cols = landed.shape[1]
    per_dev = snaps // cols
    chips = n_snap // 2

    i = lax.axis_index("space")
    s = lax.axis_index("snap")
    odd = lax.rem(i, 2)
    core = lax.rem(s, 2)
    chip = s // 2
    partner = i + 1 - 2 * odd
    ahead = lax.rem(i + 2 - 4 * odd + n_space, n_space)
    behind = lax.rem(i - 2 + 4 * odd + n_space, n_space)
    mate = s + 1 - 2 * core

    def peer(o):
        return 2 * lax.rem(chip + o, chips) + core

    def origin(o):
        return 2 * lax.rem(chip + chips - o, chips) + core

    barrier = pltpu.get_barrier_semaphore()

    def signal(sem, **where):
        pl.semaphore_signal(sem, inc=1, device_id=where, device_id_type=pl.DeviceIdType.MESH)

    signal(barrier, space=partner)
    signal(barrier, space=ahead)
    signal(barrier, space=behind)
    signal(barrier, snap=mate)
    for o in range(1, chips):
        signal(barrier, snap=peer(o))
    pl.semaphore_wait(barrier, 3 + chips)

    def rows(t):
        return pl.ds(pl.multiple_of(t * ROWS, ROWS), ROWS)

    def part(p):
        return pl.ds(p * cells, cells)

    def x_copy(t, p):
        where = (rows(t), part(p))
        return remote(u_ref.at[where], side.at[where], x_s.at[t, p], x_r.at[t, p], space=partner)

    def z_copy(t, p):
        block = (rows(t), part(p))
        return remote(side.at[block], far.at[block], z_s.at[t, p], z_r.at[t, p], space=ahead)

    def m_copy(t):
        block = gathered.at[s, rows(t)]
        return remote(block, block, m_s.at[t], m_r.at[t], snap=mate)

    def m_arrival(t):
        block = gathered.at[mate, rows(t)]
        return remote(block, block, m_s.at[t], m_r.at[t], snap=mate)

    def cross(source, o, t, p):
        block = gathered.at[source, rows(t), part(p)]
        return remote(block, block, y_s.at[o - 1, t, p], y_r.at[o - 1, t, p], snap=peer(o))

    def y_copy(o, t, p):
        return cross(s, o, t, p)

    def y_arrival(o, t, p):
        return cross(origin(o), o, t, p)

    def onward(source, o, t, p):
        block = gathered.at[source, rows(t), part(p)]
        return remote(block, block, f_s.at[o - 1, t, p], f_r.at[o - 1, t, p], snap=mate)

    def f_copy(o, t, p):
        return onward(origin(o), o, t, p)

    def f_origin(o):
        return 2 * lax.rem(chip + chips - o, chips) + 1 - core

    def f_arrival(o, t, p):
        return onward(f_origin(o), o, t, p)

    lane = lax.rem(lax.broadcasted_iota(jnp.int32, (ROWS, cells), 1), 128)
    sign = (1 - 2 * odd).astype(jnp.float32)

    def vorticity(t):
        d_i, d_j, d_k = [], [], []
        for c in range(3):
            here = u_ref[rows(t), part(c)].astype(jnp.float32)
            near = side[rows(t), part(c)].astype(jnp.float32)
            away = far[rows(t), part(c)].astype(jnp.float32)
            d_i.append((near - away) * sign)
            edge = jnp.zeros((ROWS, 128), jnp.float32)
            d_j.append(
                jnp.concatenate([here[:, 128:], edge], axis=1)
                - jnp.concatenate([edge, here[:, :-128]], axis=1)
            )
            d_k.append(
                jnp.where(lane == 127, 0.0, pltpu.roll(here, cells - 1, 1))
                - jnp.where(lane == 0, 0.0, pltpu.roll(here, 1, 1))
            )

        def deriv(comp, a):
            return (
                coef_ref[pl.ds(3 * a, 1), :] * d_i[comp]
                + coef_ref[pl.ds(3 * a + 1, 1), :] * d_j[comp]
                + coef_ref[pl.ds(3 * a + 2, 1), :] * d_k[comp]
            )

        for c, (p, q) in enumerate(((2, 1), (0, 2), (1, 0))):
            gathered[s, rows(t), part(c)] = (
                deriv(p, q) - deriv(q, p)
            ).astype(jnp.bfloat16)

    def launch(t, carry):
        for p in range(3):
            x_copy(t, p).start()
        return carry

    lax.fori_loop(0, chunks, launch, 0)

    rounds = n_space // 4 - 1
    signal(ring.at[0, 0], space=ahead)
    signal(ring.at[0, 1], space=behind)

    for j in range(cells // 128):
        line = pl.ds(j, 1)
        weight = 0.5 * jnp.sqrt(volume_ref[line, :] * mask_ref[0, j].astype(jnp.float32))
        coef_ref[:, pl.ds(j * 128, 128)] = metric_ref[:, j, :] * weight

    def step(t, carry):
        @pl.when(t < chunks)
        def _():
            for p in range(3):
                x_copy(t, p).wait_recv()
                z_copy(t, p).start()

        @pl.when(jnp.logical_and(t >= 1, t < chunks + 1))
        def _():
            for p in range(3):
                z_copy(t - 1, p).wait_recv()
            vorticity(t - 1)
            for p in range(3):
                for o in range(1, chips):
                    y_copy(o, t - 1, p).start()
            m_copy(t - 1).start()

        @pl.when(t >= 3)
        def _():
            for p in range(3):
                for o in range(1, chips):
                    y_arrival(o, t - 3, p).wait_recv()
                    f_copy(o, t - 3, p).start()

        return carry

    def r_copy(block):
        return remote(
            partial.at[block], landed.at[i], r_s.at[block], r_r.at[i], space=block
        )

    def r_arrival(source):
        return remote(
            partial.at[i], landed.at[source], r_s.at[source], r_r.at[source], space=source
        )

    def product(dev, h):
        block = dev * per_dev + h
        partial[block] = lax.dot_general(
            gathered[dev, pl.ds(h * cols, cols), :], gathered[s], (((1,), (1,)), ((), ())),
            preferred_element_type=jnp.float32,
        )

        @pl.when(block != i)
        def _():
            r_copy(block).start()

    def await_m(t, carry):
        m_arrival(t).wait_recv()
        return carry

    per_block = cols // ROWS

    def product_f(o, h):
        def await_f(t, carry):
            for p in range(3):
                f_arrival(o, t, p).wait_recv()
            return carry

        lax.fori_loop(h * per_block, (h + 1) * per_block, await_f, 0)
        product(f_origin(o), h)

    lax.fori_loop(0, chunks // 2, step, 0)
    for n in range(rounds):
        pl.semaphore_wait(ring.at[n, 0], 1)
        pl.semaphore_wait(ring.at[n, 1], 1)
        if n < rounds - 1:
            signal(ring.at[n + 1, 0], space=ahead)
            signal(ring.at[n + 1, 1], space=behind)
    signal(pair, space=partner)
    lax.fori_loop(chunks // 2, chunks + 1, step, 0)
    pl.semaphore_wait(pair, 1)
    for h in range(per_dev):
        product(s, h)
    lax.fori_loop(0, chunks, await_m, 0)
    for h in range(per_dev):
        product(mate, h)
    lax.fori_loop(chunks + 1, chunks + 2, step, 0)
    for o in range(1, chips):
        for h in range(per_dev - 1):
            product(origin(o), h)
    lax.fori_loop(chunks + 2, chunks + 3, step, 0)
    for o in range(1, chips):
        for h in range(per_dev - 1):
            product_f(o, h)
    for o in range(1, chips):
        product(origin(o), per_dev - 1)
    for o in range(1, chips):
        product_f(o, per_dev - 1)

    def add(d, total):
        source = lax.rem(i + d, n_space)
        r_arrival(source).wait_recv()
        return total + landed[source]

    total = lax.fori_loop(1, n_space, add, partial[i])
    out_ref[...] = total

    def drain(t, carry):
        m_copy(t).wait_send()
        for p in range(3):
            x_copy(t, p).wait_send()
            z_copy(t, p).wait_send()
            for o in range(1, chips):
                y_copy(o, t, p).wait_send()
                f_copy(o, t, p).wait_send()
        return carry

    lax.fori_loop(0, chunks, drain, 0)

    def drain_r(d, carry):
        r_copy(lax.rem(i + d, n_space)).wait_send()
        return carry

    lax.fori_loop(1, n_space, drain_r, 0)


def shards(n_space, n_snap, velocity, metric, volume, blade_mask):
    snaps = velocity.shape[0]
    u = velocity.reshape(snaps, -1)
    width = u.shape[1]
    cols = snaps * n_snap // n_space
    chunks = snaps // ROWS
    chips = n_snap // 2
    far = max(chips - 1, 1)
    dma = pltpu.SemaphoreType.DMA
    return pl.pallas_call(
        functools.partial(kernel, n_space, n_snap),
        out_shape=jax.ShapeDtypeStruct((cols, snaps), jnp.float32),
        in_specs=[pl.BlockSpec(memory_space=pltpu.VMEM)] * 3
        + [pl.BlockSpec(memory_space=pltpu.SMEM)],
        out_specs=pl.BlockSpec(memory_space=pltpu.VMEM),
        scratch_shapes=[
            pltpu.VMEM((9, width // 3), jnp.float32),
            pltpu.VMEM((snaps, width), jnp.bfloat16),
            pltpu.VMEM((snaps, width), jnp.bfloat16),
            pltpu.VMEM((n_snap, snaps, width), jnp.bfloat16),
            pltpu.VMEM((n_space, cols, snaps), jnp.float32),
            pltpu.VMEM((n_space, cols, snaps), jnp.float32),
            dma((chunks, 3)), dma((chunks, 3)), dma((chunks, 3)), dma((chunks, 3)),
            dma((chunks,)), dma((chunks,)),
            dma((far, chunks, 3)), dma((far, chunks, 3)),
            dma((far, chunks, 3)), dma((far, chunks, 3)),
            dma((n_space,)), dma((n_space,)),
            pltpu.SemaphoreType.REGULAR((n_space // 4 - 1, 2)), pltpu.SemaphoreType.REGULAR,
        ],
        compiler_params=pltpu.CompilerParams(
            collective_id=0, has_side_effects=True, vmem_limit_bytes=48 * 1024 * 1024
        ),
    )(u, metric[:, 0], volume[0], blade_mask).T


def solution(mesh):
    in_specs = (
        P("snap", None, "space", None, None),
        P(None, "space", None, None),
        P("space", None, None),
        P("space", None),
    )
    body = functools.partial(shards, mesh.shape["space"], mesh.shape["snap"])
    return jax.shard_map(body, mesh=mesh, in_specs=in_specs, out_specs=P("snap", "space"), check_vma=False)
```

```python
import functools

import jax
import jax.numpy as jnp
from jax import lax
from jax.experimental import pallas as pl
from jax.experimental.pallas import tpu as pltpu
from jax.sharding import PartitionSpec as P

ROWS = 16
PIECE = 32


def remote(src, dst, send_sem, recv_sem, **where):
    return pltpu.make_async_remote_copy(
        src_ref=src,
        dst_ref=dst,
        send_sem=send_sem,
        recv_sem=recv_sem,
        device_id=where,
        device_id_type=pl.DeviceIdType.MESH,
    )


def kernel(
    n_space, n_snap, u_ref, metric_ref, volume_ref, mask_ref, out_ref,
    coef_ref, side, far, gathered, partial, landed,
    x_s, x_r, z_s, z_r, m_s, m_r, y_s, y_r, f_s, f_r, r_s, r_r, flags, mask_sem,
):
    snaps, width = u_ref.shape
    cells = width // 3
    chunks = snaps // ROWS
    cols = landed.shape[1]
    per_dev = snaps // cols
    chips = n_snap // 2

    i = lax.axis_index("space")
    s = lax.axis_index("snap")
    odd = lax.rem(i, 2)
    core = lax.rem(s, 2)
    chip = s // 2
    partner = i + 1 - 2 * odd
    ahead = lax.rem(i + 2 - 4 * odd + n_space, n_space)
    mate = s + 1 - 2 * core

    def peer(o):
        return 2 * lax.rem(chip + o, chips) + core

    def origin(o):
        return 2 * lax.rem(chip + chips - o, chips) + core

    mask_copy = pltpu.make_async_copy(mask_ref, flags, mask_sem)
    mask_copy.start()
    barrier = pltpu.get_barrier_semaphore()

    def greet(d, carry):
        pl.semaphore_signal(
            barrier, inc=1, device_id={"space": lax.rem(i + d, n_space)},
            device_id_type=pl.DeviceIdType.MESH,
        )
        return carry

    lax.fori_loop(1, n_space, greet, 0)
    pl.semaphore_signal(
        barrier, inc=1, device_id={"snap": mate}, device_id_type=pl.DeviceIdType.MESH
    )
    for o in range(1, chips):
        pl.semaphore_signal(
            barrier, inc=1, device_id={"snap": peer(o)}, device_id_type=pl.DeviceIdType.MESH
        )
    pl.semaphore_wait(barrier, n_space - 1 + chips)

    def rows(t):
        return pl.ds(pl.multiple_of(t * ROWS, ROWS), ROWS)

    def part(p):
        return pl.ds(p * cells, cells)

    def x_copy(t, p):
        where = (rows(t), part(p))
        return remote(u_ref.at[where], side.at[where], x_s.at[t, p], x_r.at[t, p], space=partner)

    def z_copy(t, p):
        block = (rows(t), part(p))
        return remote(side.at[block], far.at[block], z_s.at[t, p], z_r.at[t, p], space=ahead)

    def m_copy(t):
        block = gathered.at[s, rows(t)]
        return remote(block, block, m_s.at[t], m_r.at[t], snap=mate)

    def m_arrival(t):
        block = gathered.at[mate, rows(t)]
        return remote(block, block, m_s.at[t], m_r.at[t], snap=mate)

    def cross(source, o, t, p):
        block = gathered.at[source, rows(t), part(p)]
        return remote(block, block, y_s.at[o - 1, t, p], y_r.at[o - 1, t, p], snap=peer(o))

    def y_copy(o, t, p):
        return cross(s, o, t, p)

    def y_arrival(o, t, p):
        return cross(origin(o), o, t, p)

    def onward(source, o, t, p):
        block = gathered.at[source, rows(t), part(p)]
        return remote(block, block, f_s.at[o - 1, t, p], f_r.at[o - 1, t, p], snap=mate)

    def f_copy(o, t, p):
        return onward(origin(o), o, t, p)

    def f_origin(o):
        return 2 * lax.rem(chip + chips - o, chips) + 1 - core

    def f_arrival(o, t, p):
        return onward(f_origin(o), o, t, p)

    lane = lax.rem(lax.broadcasted_iota(jnp.int32, (ROWS, cells), 1), 128)
    sign = (1 - 2 * odd).astype(jnp.float32)

    def vorticity(t):
        d_i, d_j, d_k = [], [], []
        for c in range(3):
            here = u_ref[rows(t), part(c)].astype(jnp.float32)
            near = side[rows(t), part(c)].astype(jnp.float32)
            away = far[rows(t), part(c)].astype(jnp.float32)
            d_i.append((near - away) * sign)
            edge = jnp.zeros((ROWS, 128), jnp.float32)
            d_j.append(
                jnp.concatenate([here[:, 128:], edge], axis=1)
                - jnp.concatenate([edge, here[:, :-128]], axis=1)
            )
            d_k.append(
                jnp.where(lane == 127, 0.0, pltpu.roll(here, cells - 1, 1))
                - jnp.where(lane == 0, 0.0, pltpu.roll(here, 1, 1))
            )

        def deriv(comp, a):
            return (
                coef_ref[pl.ds(3 * a, 1), :] * d_i[comp]
                + coef_ref[pl.ds(3 * a + 1, 1), :] * d_j[comp]
                + coef_ref[pl.ds(3 * a + 2, 1), :] * d_k[comp]
            )

        for c, (p, q) in enumerate(((2, 1), (0, 2), (1, 0))):
            gathered[s, rows(t), part(c)] = (
                deriv(p, q) - deriv(q, p)
            ).astype(jnp.bfloat16)

    def launch(t, carry):
        for p in range(3):
            x_copy(t, p).start()
        return carry

    lax.fori_loop(0, chunks, launch, 0)

    mask_copy.wait()
    for j in range(cells // 128):
        line = pl.ds(j, 1)
        weight = 0.5 * jnp.sqrt(volume_ref[line, :] * flags[0, j].astype(jnp.float32))
        coef_ref[:, pl.ds(j * 128, 128)] = metric_ref[:, j, :] * weight

    def step(t, carry):
        @pl.when(t < chunks)
        def _():
            for p in range(3):
                x_copy(t, p).wait_recv()
                z_copy(t, p).start()

        @pl.when(jnp.logical_and(t >= 1, t < chunks + 1))
        def _():
            for p in range(3):
                z_copy(t - 1, p).wait_recv()
            vorticity(t - 1)
            for p in range(3):
                for o in range(1, chips):
                    y_copy(o, t - 1, p).start()
            m_copy(t - 1).start()

        @pl.when(t >= 3)
        def _():
            for p in range(3):
                for o in range(1, chips):
                    y_arrival(o, t - 3, p).wait_recv()
                    f_copy(o, t - 3, p).start()

        return carry

    def r_copy(block, q):
        piece = pl.ds(q * PIECE, PIECE)
        return remote(
            partial.at[block, piece], landed.at[i, piece],
            r_s.at[block, q], r_r.at[i, q], space=block,
        )

    def r_arrival(source, q):
        piece = pl.ds(q * PIECE, PIECE)
        return remote(
            partial.at[i, piece], landed.at[source, piece],
            r_s.at[source, q], r_r.at[source, q], space=source,
        )

    per_block = cols // PIECE
    per_piece = PIECE // ROWS
    pieces = snaps // PIECE

    def product(dev, n):
        block = dev * per_dev + n // per_block
        q = n % per_block
        partial[block, pl.ds(q * PIECE, PIECE)] = lax.dot_general(
            gathered[dev, pl.ds(n * PIECE, PIECE), :], gathered[s], (((1,), (1,)), ((), ())),
            preferred_element_type=jnp.float32,
        )

        @pl.when(block != i)
        def _():
            r_copy(block, q).start()

    def await_m(t, carry):
        m_arrival(t).wait_recv()
        return carry

    def product_f(o, n):
        def await_f(t, carry):
            for p in range(3):
                f_arrival(o, t, p).wait_recv()
            return carry

        lax.fori_loop(n * per_piece, (n + 1) * per_piece, await_f, 0)
        product(f_origin(o), n)

    lax.fori_loop(0, chunks + 1, step, 0)
    for n in range(pieces):
        product(s, n)
    lax.fori_loop(0, chunks, await_m, 0)
    for n in range(pieces):
        product(mate, n)
    lax.fori_loop(chunks + 1, chunks + 2, step, 0)
    for o in range(1, chips):
        for n in range(pieces - 1):
            product(origin(o), n)
        for n in range(pieces - 1):
            product_f(o, n)
    lax.fori_loop(chunks + 2, chunks + 3, step, 0)
    for o in range(1, chips):
        product(origin(o), pieces - 1)
    for o in range(1, chips):
        product_f(o, pieces - 1)

    def add(d, total):
        source = lax.rem(i + d, n_space)
        for q in range(per_block):
            r_arrival(source, q).wait_recv()
        return total + landed[source]

    out_ref[...] = lax.fori_loop(1, n_space, add, partial[i])

    def drain(t, carry):
        m_copy(t).wait_send()
        for p in range(3):
            x_copy(t, p).wait_send()
            z_copy(t, p).wait_send()
            for o in range(1, chips):
                y_copy(o, t, p).wait_send()
                f_copy(o, t, p).wait_send()
        return carry

    lax.fori_loop(0, chunks, drain, 0)

    def drain_r(d, carry):
        for q in range(per_block):
            r_copy(lax.rem(i + d, n_space), q).wait_send()
        return carry

    lax.fori_loop(1, n_space, drain_r, 0)


def shards(n_space, n_snap, velocity, metric, volume, blade_mask):
    snaps = velocity.shape[0]
    u = velocity.reshape(snaps, -1)
    width = u.shape[1]
    cols = snaps * n_snap // n_space
    chunks = snaps // ROWS
    chips = n_snap // 2
    far = max(chips - 1, 1)
    dma = pltpu.SemaphoreType.DMA
    return pl.pallas_call(
        functools.partial(kernel, n_space, n_snap),
        out_shape=jax.ShapeDtypeStruct((cols, snaps), jnp.float32),
        in_specs=[pl.BlockSpec(memory_space=pltpu.VMEM)] * 3
        + [pl.BlockSpec(memory_space=pltpu.HBM)],
        out_specs=pl.BlockSpec(memory_space=pltpu.VMEM),
        scratch_shapes=[
            pltpu.VMEM((9, width // 3), jnp.float32),
            pltpu.VMEM((snaps, width), jnp.bfloat16),
            pltpu.VMEM((snaps, width), jnp.bfloat16),
            pltpu.VMEM((n_snap, snaps, width), jnp.bfloat16),
            pltpu.VMEM((n_space, cols, snaps), jnp.float32),
            pltpu.VMEM((n_space, cols, snaps), jnp.float32),
            dma((chunks, 3)), dma((chunks, 3)), dma((chunks, 3)), dma((chunks, 3)),
            dma((chunks,)), dma((chunks,)),
            dma((far, chunks, 3)), dma((far, chunks, 3)),
            dma((far, chunks, 3)), dma((far, chunks, 3)),
            dma((n_space, cols // PIECE)), dma((n_space, cols // PIECE)),
            pltpu.SMEM(blade_mask.shape, jnp.int32), dma,
        ],
        compiler_params=pltpu.CompilerParams(
            collective_id=0, has_side_effects=True, vmem_limit_bytes=48 * 1024 * 1024
        ),
    )(u, metric[:, 0], volume[0], blade_mask).T


def solution(mesh):
    in_specs = (
        P("snap", None, "space", None, None),
        P(None, "space", None, None),
        P("space", None, None),
        P("space", None),
    )
    body = functools.partial(shards, mesh.shape["space"], mesh.shape["snap"])
    return jax.shard_map(body, mesh=mesh, in_specs=in_specs, out_specs=P("snap", "space"), check_vma=False)
```

```python
import functools

import jax
import jax.numpy as jnp
from jax import lax
from jax.experimental import pallas as pl
from jax.experimental.pallas import tpu as pltpu
from jax.sharding import PartitionSpec as P

ROWS = 16
Z_LAG = 2
Y_LAG = 4


def remote(src, dst, send_sem, recv_sem, **where):
    return pltpu.make_async_remote_copy(
        src_ref=src,
        dst_ref=dst,
        send_sem=send_sem,
        recv_sem=recv_sem,
        device_id=where,
        device_id_type=pl.DeviceIdType.MESH,
    )


def kernel(
    n_space, n_snap, u_ref, metric_ref, volume_ref, mask_ref, out_ref,
    coef_ref, side, far, gathered, partial, landed,
    x_s, x_r, z_s, z_r, m_s, m_r, y_s, y_r, f_s, f_r, r_s, r_r, flags, mask_sem,
):
    snaps, width = u_ref.shape
    cells = width // 3
    chunks = snaps // ROWS
    cols = landed.shape[1]
    per_dev = snaps // cols
    chips = n_snap // 2

    i = lax.axis_index("space")
    s = lax.axis_index("snap")
    odd = lax.rem(i, 2)
    core = lax.rem(s, 2)
    chip = s // 2
    partner = i + 1 - 2 * odd
    ahead = lax.rem(i + 2 - 4 * odd + n_space, n_space)
    mate = s + 1 - 2 * core

    def peer(o):
        return 2 * lax.rem(chip + o, chips) + core

    def origin(o):
        return 2 * lax.rem(chip + chips - o, chips) + core

    mask_copy = pltpu.make_async_copy(mask_ref, flags, mask_sem)
    mask_copy.start()
    barrier = pltpu.get_barrier_semaphore()

    def greet(d, carry):
        pl.semaphore_signal(
            barrier, inc=1, device_id={"space": lax.rem(i + d, n_space)},
            device_id_type=pl.DeviceIdType.MESH,
        )
        return carry

    lax.fori_loop(1, n_space, greet, 0)
    pl.semaphore_signal(
        barrier, inc=1, device_id={"snap": mate}, device_id_type=pl.DeviceIdType.MESH
    )
    for o in range(1, chips):
        pl.semaphore_signal(
            barrier, inc=1, device_id={"snap": peer(o)}, device_id_type=pl.DeviceIdType.MESH
        )
    pl.semaphore_wait(barrier, n_space - 1 + chips)

    def rows(t):
        return pl.ds(pl.multiple_of(t * ROWS, ROWS), ROWS)

    def part(p):
        return pl.ds(p * cells, cells)

    def x_copy(t, p):
        where = (rows(t), part(p))
        return remote(u_ref.at[where], side.at[where], x_s.at[t, p], x_r.at[t, p], space=partner)

    def z_copy(t, p):
        block = (rows(t), part(p))
        return remote(side.at[block], far.at[block], z_s.at[t, p], z_r.at[t, p], space=ahead)

    def m_copy(t):
        block = gathered.at[s, rows(t)]
        return remote(block, block, m_s.at[t], m_r.at[t], snap=mate)

    def m_arrival(t):
        block = gathered.at[mate, rows(t)]
        return remote(block, block, m_s.at[t], m_r.at[t], snap=mate)

    def cross(source, o, t, p):
        block = gathered.at[source, rows(t), part(p)]
        return remote(block, block, y_s.at[o - 1, t, p], y_r.at[o - 1, t, p], snap=peer(o))

    def y_copy(o, t, p):
        return cross(s, o, t, p)

    def y_arrival(o, t, p):
        return cross(origin(o), o, t, p)

    def onward(source, o, t, p):
        block = gathered.at[source, rows(t), part(p)]
        return remote(block, block, f_s.at[o - 1, t, p], f_r.at[o - 1, t, p], snap=mate)

    def f_copy(o, t, p):
        return onward(origin(o), o, t, p)

    def f_origin(o):
        return 2 * lax.rem(chip + chips - o, chips) + 1 - core

    def f_arrival(o, t, p):
        return onward(f_origin(o), o, t, p)

    lane = lax.rem(lax.broadcasted_iota(jnp.int32, (ROWS, cells), 1), 128)
    sign = (1 - 2 * odd).astype(jnp.float32)

    def vorticity(t):
        d_i, d_j, d_k = [], [], []
        for c in range(3):
            here = u_ref[rows(t), part(c)].astype(jnp.float32)
            near = side[rows(t), part(c)].astype(jnp.float32)
            away = far[rows(t), part(c)].astype(jnp.float32)
            d_i.append((near - away) * sign)
            edge = jnp.zeros((ROWS, 128), jnp.float32)
            d_j.append(
                jnp.concatenate([here[:, 128:], edge], axis=1)
                - jnp.concatenate([edge, here[:, :-128]], axis=1)
            )
            d_k.append(
                jnp.where(lane == 127, 0.0, pltpu.roll(here, cells - 1, 1))
                - jnp.where(lane == 0, 0.0, pltpu.roll(here, 1, 1))
            )

        def deriv(comp, a):
            return (
                coef_ref[pl.ds(3 * a, 1), :] * d_i[comp]
                + coef_ref[pl.ds(3 * a + 1, 1), :] * d_j[comp]
                + coef_ref[pl.ds(3 * a + 2, 1), :] * d_k[comp]
            )

        for c, (p, q) in enumerate(((2, 1), (0, 2), (1, 0))):
            gathered[s, rows(t), part(c)] = (
                deriv(p, q) - deriv(q, p)
            ).astype(jnp.bfloat16)

    def launch(t, carry):
        for p in range(3):
            x_copy(t, p).start()
        return carry

    lax.fori_loop(0, chunks, launch, 0)

    mask_copy.wait()
    for j in range(cells // 128):
        line = pl.ds(j, 1)
        weight = 0.5 * jnp.sqrt(volume_ref[line, :] * flags[0, j].astype(jnp.float32))
        coef_ref[:, pl.ds(j * 128, 128)] = metric_ref[:, j, :] * weight

    def step(t, carry):
        @pl.when(t < chunks)
        def _():
            for p in range(3):
                x_copy(t, p).wait_recv()
                z_copy(t, p).start()

        @pl.when(jnp.logical_and(t >= Z_LAG, t < chunks + Z_LAG))
        def _():
            for p in range(3):
                z_copy(t - Z_LAG, p).wait_recv()
            vorticity(t - Z_LAG)
            for p in range(3):
                for o in range(1, chips):
                    y_copy(o, t - Z_LAG, p).start()
            m_copy(t - Z_LAG).start()

        @pl.when(t >= Y_LAG)
        def _():
            for p in range(3):
                for o in range(1, chips):
                    y_arrival(o, t - Y_LAG, p).wait_recv()
                    f_copy(o, t - Y_LAG, p).start()

        return carry

    def r_copy(block):
        return remote(
            partial.at[block], landed.at[i], r_s.at[block], r_r.at[i], space=block
        )

    def r_arrival(source):
        return remote(
            partial.at[i], landed.at[source], r_s.at[source], r_r.at[source], space=source
        )

    def product(dev, h):
        block = dev * per_dev + h
        partial[block] = lax.dot_general(
            gathered[dev, pl.ds(h * cols, cols), :], gathered[s], (((1,), (1,)), ((), ())),
            preferred_element_type=jnp.float32,
        )

        @pl.when(block != i)
        def _():
            r_copy(block).start()

    def await_m(t, carry):
        m_arrival(t).wait_recv()
        return carry

    per_block = cols // ROWS

    def product_f(o, h):
        def await_f(t, carry):
            for p in range(3):
                f_arrival(o, t, p).wait_recv()
            return carry

        lax.fori_loop(h * per_block, (h + 1) * per_block, await_f, 0)
        product(f_origin(o), h)

    def whole_product(dev):
        result = lax.dot_general(
            gathered[dev], gathered[s], (((1,), (1,)), ((), ())),
            preferred_element_type=jnp.float32,
        )
        for h in range(per_dev):
            block = dev * per_dev + h
            partial[block] = result[h * cols:(h + 1) * cols]

            @pl.when(block != i)
            def _():
                r_copy(block).start()

    done = chunks + Z_LAG
    lax.fori_loop(0, done, step, 0)
    whole_product(s)
    lax.fori_loop(0, chunks, await_m, 0)
    whole_product(mate)
    lax.fori_loop(done, chunks + Y_LAG - 1, step, 0)
    for o in range(1, chips):
        for h in range(per_dev - 1):
            product(origin(o), h)
    lax.fori_loop(chunks + Y_LAG - 1, chunks + Y_LAG, step, 0)
    for o in range(1, chips):
        for h in range(per_dev - 1):
            product_f(o, h)
    for o in range(1, chips):
        product(origin(o), per_dev - 1)
    for o in range(1, chips):
        product_f(o, per_dev - 1)

    def add(d, total):
        source = lax.rem(i + d, n_space)
        r_arrival(source).wait_recv()
        return total + landed[source]

    total = lax.fori_loop(1, n_space, add, partial[i])
    out_ref[...] = total

    def drain(t, carry):
        m_copy(t).wait_send()
        for p in range(3):
            x_copy(t, p).wait_send()
            z_copy(t, p).wait_send()
            for o in range(1, chips):
                y_copy(o, t, p).wait_send()
                f_copy(o, t, p).wait_send()
        return carry

    lax.fori_loop(0, chunks, drain, 0)

    def drain_r(d, carry):
        r_copy(lax.rem(i + d, n_space)).wait_send()
        return carry

    lax.fori_loop(1, n_space, drain_r, 0)


def shards(n_space, n_snap, velocity, metric, volume, blade_mask):
    snaps = velocity.shape[0]
    u = velocity.reshape(snaps, -1)
    width = u.shape[1]
    cols = snaps * n_snap // n_space
    chunks = snaps // ROWS
    chips = n_snap // 2
    far = max(chips - 1, 1)
    dma = pltpu.SemaphoreType.DMA
    return pl.pallas_call(
        functools.partial(kernel, n_space, n_snap),
        out_shape=jax.ShapeDtypeStruct((cols, snaps), jnp.float32),
        in_specs=[pl.BlockSpec(memory_space=pltpu.VMEM)] * 3
        + [pl.BlockSpec(memory_space=pltpu.HBM)],
        out_specs=pl.BlockSpec(memory_space=pltpu.VMEM),
        scratch_shapes=[
            pltpu.VMEM((9, width // 3), jnp.float32),
            pltpu.VMEM((snaps, width), jnp.bfloat16),
            pltpu.VMEM((snaps, width), jnp.bfloat16),
            pltpu.VMEM((n_snap, snaps, width), jnp.bfloat16),
            pltpu.VMEM((n_space, cols, snaps), jnp.float32),
            pltpu.VMEM((n_space, cols, snaps), jnp.float32),
            dma((chunks, 3)), dma((chunks, 3)), dma((chunks, 3)), dma((chunks, 3)),
            dma((chunks,)), dma((chunks,)),
            dma((far, chunks, 3)), dma((far, chunks, 3)),
            dma((far, chunks, 3)), dma((far, chunks, 3)),
            dma((n_space,)), dma((n_space,)),
            pltpu.SMEM(blade_mask.shape, jnp.int32), dma,
        ],
        compiler_params=pltpu.CompilerParams(
            collective_id=0, has_side_effects=True, vmem_limit_bytes=48 * 1024 * 1024
        ),
    )(u, metric[:, 0], volume[0], blade_mask).T


def solution(mesh):
    in_specs = (
        P("snap", None, "space", None, None),
        P(None, "space", None, None),
        P("space", None, None),
        P("space", None),
    )
    body = functools.partial(shards, mesh.shape["space"], mesh.shape["snap"])
    return jax.shard_map(body, mesh=mesh, in_specs=in_specs, out_specs=P("snap", "space"), check_vma=False)
```

```python
import functools

import jax
import jax.numpy as jnp
from jax import lax
from jax.experimental import pallas as pl
from jax.experimental.pallas import tpu as pltpu
from jax.sharding import PartitionSpec as P

ROWS = 16
Z_LAG = 2
Y_LAG = 4


def remote(src, dst, send_sem, recv_sem, **where):
    return pltpu.make_async_remote_copy(
        src_ref=src,
        dst_ref=dst,
        send_sem=send_sem,
        recv_sem=recv_sem,
        device_id=where,
        device_id_type=pl.DeviceIdType.MESH,
    )


def kernel(
    n_space, n_snap, u_ref, metric_ref, volume_ref, mask_ref, out_ref,
    coef_ref, side, far, gathered, partial, landed,
    x_s, x_r, z_s, z_r, m_s, m_r, y_s, y_r, f_s, f_r, r_s, r_r, flags, mask_sem, ring, pair,
):
    snaps, width = u_ref.shape
    cells = width // 3
    chunks = snaps // ROWS
    cols = landed.shape[1]
    per_dev = snaps // cols
    chips = n_snap // 2

    i = lax.axis_index("space")
    s = lax.axis_index("snap")
    odd = lax.rem(i, 2)
    core = lax.rem(s, 2)
    chip = s // 2
    partner = i + 1 - 2 * odd
    ahead = lax.rem(i + 2 - 4 * odd + n_space, n_space)
    behind = lax.rem(i - 2 + 4 * odd + n_space, n_space)
    mate = s + 1 - 2 * core

    def peer(o):
        return 2 * lax.rem(chip + o, chips) + core

    def origin(o):
        return 2 * lax.rem(chip + chips - o, chips) + core

    mask_copy = pltpu.make_async_copy(mask_ref, flags, mask_sem)
    mask_copy.start()
    barrier = pltpu.get_barrier_semaphore()

    def signal(sem, **where):
        pl.semaphore_signal(sem, inc=1, device_id=where, device_id_type=pl.DeviceIdType.MESH)

    signal(barrier, space=partner)
    signal(barrier, space=ahead)
    signal(barrier, space=behind)
    signal(barrier, snap=mate)
    for o in range(1, chips):
        signal(barrier, snap=peer(o))
    pl.semaphore_wait(barrier, 3 + chips)

    def rows(t):
        return pl.ds(pl.multiple_of(t * ROWS, ROWS), ROWS)

    def part(p):
        return pl.ds(p * cells, cells)

    def x_copy(t, p):
        where = (rows(t), part(p))
        return remote(u_ref.at[where], side.at[where], x_s.at[t, p], x_r.at[t, p], space=partner)

    def z_copy(t, p):
        block = (rows(t), part(p))
        return remote(side.at[block], far.at[block], z_s.at[t, p], z_r.at[t, p], space=ahead)

    def m_copy(t):
        block = gathered.at[s, rows(t)]
        return remote(block, block, m_s.at[t], m_r.at[t], snap=mate)

    def m_arrival(t):
        block = gathered.at[mate, rows(t)]
        return remote(block, block, m_s.at[t], m_r.at[t], snap=mate)

    def cross(source, o, t, p):
        block = gathered.at[source, rows(t), part(p)]
        return remote(block, block, y_s.at[o - 1, t, p], y_r.at[o - 1, t, p], snap=peer(o))

    def y_copy(o, t, p):
        return cross(s, o, t, p)

    def y_arrival(o, t, p):
        return cross(origin(o), o, t, p)

    def onward(source, o, t, p):
        block = gathered.at[source, rows(t), part(p)]
        return remote(block, block, f_s.at[o - 1, t, p], f_r.at[o - 1, t, p], snap=mate)

    def f_copy(o, t, p):
        return onward(origin(o), o, t, p)

    def f_origin(o):
        return 2 * lax.rem(chip + chips - o, chips) + 1 - core

    def f_arrival(o, t, p):
        return onward(f_origin(o), o, t, p)

    lane = lax.rem(lax.broadcasted_iota(jnp.int32, (ROWS, cells), 1), 128)
    sign = (1 - 2 * odd).astype(jnp.float32)

    def vorticity(t):
        d_i, d_j, d_k = [], [], []
        for c in range(3):
            here = u_ref[rows(t), part(c)].astype(jnp.float32)
            near = side[rows(t), part(c)].astype(jnp.float32)
            away = far[rows(t), part(c)].astype(jnp.float32)
            d_i.append((near - away) * sign)
            edge = jnp.zeros((ROWS, 128), jnp.float32)
            d_j.append(
                jnp.concatenate([here[:, 128:], edge], axis=1)
                - jnp.concatenate([edge, here[:, :-128]], axis=1)
            )
            d_k.append(
                jnp.where(lane == 127, 0.0, pltpu.roll(here, cells - 1, 1))
                - jnp.where(lane == 0, 0.0, pltpu.roll(here, 1, 1))
            )

        def deriv(comp, a):
            return (
                coef_ref[pl.ds(3 * a, 1), :] * d_i[comp]
                + coef_ref[pl.ds(3 * a + 1, 1), :] * d_j[comp]
                + coef_ref[pl.ds(3 * a + 2, 1), :] * d_k[comp]
            )

        for c, (p, q) in enumerate(((2, 1), (0, 2), (1, 0))):
            gathered[s, rows(t), part(c)] = (
                deriv(p, q) - deriv(q, p)
            ).astype(jnp.bfloat16)

    def launch(t, carry):
        for p in range(3):
            x_copy(t, p).start()
        return carry

    lax.fori_loop(0, chunks, launch, 0)

    rounds = n_space // 4 - 1
    signal(ring.at[0, 0], space=ahead)
    signal(ring.at[0, 1], space=behind)
    mask_copy.wait()
    for j in range(cells // 128):
        line = pl.ds(j, 1)
        weight = 0.5 * jnp.sqrt(volume_ref[line, :] * flags[0, j].astype(jnp.float32))
        coef_ref[:, pl.ds(j * 128, 128)] = metric_ref[:, j, :] * weight

    def step(t, carry):
        def forward(parts):
            @pl.when(t < chunks)
            def _():
                for p in parts:
                    x_copy(t, p).wait_recv()
                    z_copy(t, p).start()

        forward(range(2))

        @pl.when(jnp.logical_and(t >= Z_LAG, t < chunks + Z_LAG))
        def _():
            for p in range(3):
                z_copy(t - Z_LAG, p).wait_recv()
            vorticity(t - Z_LAG)
            for p in range(3):
                for o in range(1, chips):
                    y_copy(o, t - Z_LAG, p).start()
            m_copy(t - Z_LAG).start()

        forward(range(2, 3))

        @pl.when(t >= Y_LAG)
        def _():
            for p in range(3):
                for o in range(1, chips):
                    y_arrival(o, t - Y_LAG, p).wait_recv()
                    f_copy(o, t - Y_LAG, p).start()

        return carry

    def r_copy(block):
        return remote(
            partial.at[block], landed.at[i], r_s.at[block], r_r.at[i], space=block
        )

    def r_arrival(source):
        return remote(
            partial.at[i], landed.at[source], r_s.at[source], r_r.at[source], space=source
        )

    def product(dev, h):
        block = dev * per_dev + h
        partial[block] = lax.dot_general(
            gathered[dev, pl.ds(h * cols, cols), :], gathered[s], (((1,), (1,)), ((), ())),
            preferred_element_type=jnp.float32,
        )

        @pl.when(block != i)
        def _():
            r_copy(block).start()

    def await_m(t, carry):
        m_arrival(t).wait_recv()
        return carry

    per_block = cols // ROWS

    def product_f(o, h):
        def await_f(t, carry):
            for p in range(3):
                f_arrival(o, t, p).wait_recv()
            return carry

        lax.fori_loop(h * per_block, (h + 1) * per_block, await_f, 0)
        product(f_origin(o), h)

    def whole_product(dev):
        result = lax.dot_general(
            gathered[dev], gathered[s], (((1,), (1,)), ((), ())),
            preferred_element_type=jnp.float32,
        )
        for h in range(per_dev):
            block = dev * per_dev + h
            partial[block] = result[h * cols:(h + 1) * cols]

            @pl.when(block != i)
            def _():
                r_copy(block).start()

    done = chunks + Z_LAG
    lax.fori_loop(0, chunks // 2, step, 0)
    for n in range(rounds):
        pl.semaphore_wait(ring.at[n, 0], 1)
        pl.semaphore_wait(ring.at[n, 1], 1)
        if n < rounds - 1:
            signal(ring.at[n + 1, 0], space=ahead)
            signal(ring.at[n + 1, 1], space=behind)
    signal(pair, space=partner)
    lax.fori_loop(chunks // 2, done, step, 0)
    pl.semaphore_wait(pair, 1)
    whole_product(s)
    lax.fori_loop(0, chunks, await_m, 0)
    whole_product(mate)
    lax.fori_loop(done, chunks + Y_LAG - 1, step, 0)
    for o in range(1, chips):
        for h in range(per_dev - 1):
            product(origin(o), h)
    lax.fori_loop(chunks + Y_LAG - 1, chunks + Y_LAG, step, 0)
    for o in range(1, chips):
        for h in range(per_dev - 1):
            product_f(o, h)
    for o in range(1, chips):
        product(origin(o), per_dev - 1)
    for o in range(1, chips):
        product_f(o, per_dev - 1)

    def add(d, total):
        source = lax.rem(i + d, n_space)
        r_arrival(source).wait_recv()
        return total + landed[source]

    total = lax.fori_loop(1, n_space, add, partial[i])
    out_ref[...] = total

    def drain(t, carry):
        m_copy(t).wait_send()
        for p in range(3):
            x_copy(t, p).wait_send()
            z_copy(t, p).wait_send()
            for o in range(1, chips):
                y_copy(o, t, p).wait_send()
                f_copy(o, t, p).wait_send()
        return carry

    lax.fori_loop(0, chunks, drain, 0)

    def drain_r(d, carry):
        r_copy(lax.rem(i + d, n_space)).wait_send()
        return carry

    lax.fori_loop(1, n_space, drain_r, 0)


def shards(n_space, n_snap, velocity, metric, volume, blade_mask):
    snaps = velocity.shape[0]
    u = velocity.reshape(snaps, -1)
    width = u.shape[1]
    cols = snaps * n_snap // n_space
    chunks = snaps // ROWS
    chips = n_snap // 2
    far = max(chips - 1, 1)
    dma = pltpu.SemaphoreType.DMA
    return pl.pallas_call(
        functools.partial(kernel, n_space, n_snap),
        out_shape=jax.ShapeDtypeStruct((cols, snaps), jnp.float32),
        in_specs=[pl.BlockSpec(memory_space=pltpu.VMEM)] * 3
        + [pl.BlockSpec(memory_space=pltpu.HBM)],
        out_specs=pl.BlockSpec(memory_space=pltpu.VMEM),
        scratch_shapes=[
            pltpu.VMEM((9, width // 3), jnp.float32),
            pltpu.VMEM((snaps, width), jnp.bfloat16),
            pltpu.VMEM((snaps, width), jnp.bfloat16),
            pltpu.VMEM((n_snap, snaps, width), jnp.bfloat16),
            pltpu.VMEM((n_space, cols, snaps), jnp.float32),
            pltpu.VMEM((n_space, cols, snaps), jnp.float32),
            dma((chunks, 3)), dma((chunks, 3)), dma((chunks, 3)), dma((chunks, 3)),
            dma((chunks,)), dma((chunks,)),
            dma((far, chunks, 3)), dma((far, chunks, 3)),
            dma((far, chunks, 3)), dma((far, chunks, 3)),
            dma((n_space,)), dma((n_space,)),
            pltpu.SMEM(blade_mask.shape, jnp.int32), dma,
            pltpu.SemaphoreType.REGULAR((n_space // 4 - 1, 2)), pltpu.SemaphoreType.REGULAR,
        ],
        compiler_params=pltpu.CompilerParams(
            collective_id=0, has_side_effects=True, vmem_limit_bytes=48 * 1024 * 1024
        ),
    )(u, metric[:, 0], volume[0], blade_mask).T


def solution(mesh):
    in_specs = (
        P("snap", None, "space", None, None),
        P(None, "space", None, None),
        P("space", None, None),
        P("space", None),
    )
    body = functools.partial(shards, mesh.shape["space"], mesh.shape["snap"])
    return jax.shard_map(body, mesh=mesh, in_specs=in_specs, out_specs=P("snap", "space"), check_vma=False)
```

```python
import functools

import jax
import jax.numpy as jnp
from jax import lax
from jax.experimental import pallas as pl
from jax.experimental.pallas import tpu as pltpu
from jax.sharding import PartitionSpec as P

ROWS = 16
Z_LAG = 2
Y_LAG = 4


def remote(src, dst, send_sem, recv_sem, **where):
    return pltpu.make_async_remote_copy(
        src_ref=src,
        dst_ref=dst,
        send_sem=send_sem,
        recv_sem=recv_sem,
        device_id=where,
        device_id_type=pl.DeviceIdType.MESH,
    )


def kernel(
    n_space, n_snap, u_ref, metric_ref, volume_ref, mask_ref, out_ref,
    coef_ref, side, far, gathered, partial, landed,
    x_s, x_r, z_s, z_r, m_s, m_r, y_s, y_r, f_s, f_r, r_s, r_r, flags, mask_sem, ring, pair,
):
    snaps, width = u_ref.shape
    cells = width // 3
    chunks = snaps // ROWS
    cols = landed.shape[1]
    per_dev = snaps // cols
    chips = n_snap // 2

    i = lax.axis_index("space")
    s = lax.axis_index("snap")
    odd = lax.rem(i, 2)
    core = lax.rem(s, 2)
    chip = s // 2
    partner = i + 1 - 2 * odd
    ahead = lax.rem(i + 2 - 4 * odd + n_space, n_space)
    behind = lax.rem(i - 2 + 4 * odd + n_space, n_space)
    mate = s + 1 - 2 * core

    def peer(o):
        return 2 * lax.rem(chip + o, chips) + core

    def origin(o):
        return 2 * lax.rem(chip + chips - o, chips) + core

    mask_copy = pltpu.make_async_copy(mask_ref, flags, mask_sem)
    mask_copy.start()
    barrier = pltpu.get_barrier_semaphore()

    def signal(sem, **where):
        pl.semaphore_signal(sem, inc=1, device_id=where, device_id_type=pl.DeviceIdType.MESH)

    signal(barrier, space=partner)
    signal(barrier, space=ahead)
    signal(barrier, space=behind)
    signal(barrier, snap=mate)
    for o in range(1, chips):
        signal(barrier, snap=peer(o))
    pl.semaphore_wait(barrier, 3 + chips)

    def rows(t):
        return pl.ds(pl.multiple_of(t * ROWS, ROWS), ROWS)

    def part(p):
        return pl.ds(p * cells, cells)

    def x_copy(t, p):
        where = (rows(t), part(p))
        return remote(u_ref.at[where], side.at[where], x_s.at[t, p], x_r.at[t, p], space=partner)

    def z_copy(t, p):
        block = (rows(t), part(p))
        return remote(side.at[block], far.at[block], z_s.at[t, p], z_r.at[t, p], space=ahead)

    def m_copy(t):
        block = gathered.at[s, rows(t)]
        return remote(block, block, m_s.at[t], m_r.at[t], snap=mate)

    def m_arrival(t):
        block = gathered.at[mate, rows(t)]
        return remote(block, block, m_s.at[t], m_r.at[t], snap=mate)

    def cross(source, o, t, p):
        block = gathered.at[source, rows(t), part(p)]
        return remote(block, block, y_s.at[o - 1, t, p], y_r.at[o - 1, t, p], snap=peer(o))

    def y_copy(o, t, p):
        return cross(s, o, t, p)

    def y_arrival(o, t, p):
        return cross(origin(o), o, t, p)

    def onward(source, o, t, p):
        block = gathered.at[source, rows(t), part(p)]
        return remote(block, block, f_s.at[o - 1, t, p], f_r.at[o - 1, t, p], snap=mate)

    def f_copy(o, t, p):
        return onward(origin(o), o, t, p)

    def f_origin(o):
        return 2 * lax.rem(chip + chips - o, chips) + 1 - core

    def f_arrival(o, t, p):
        return onward(f_origin(o), o, t, p)

    lane = lax.rem(lax.broadcasted_iota(jnp.int32, (ROWS, cells), 1), 128)
    sign = (1 - 2 * odd).astype(jnp.float32)

    def vorticity(t):
        d_i, d_j, d_k = [], [], []
        for c in range(3):
            here = u_ref[rows(t), part(c)].astype(jnp.float32)
            near = side[rows(t), part(c)].astype(jnp.float32)
            away = far[rows(t), part(c)].astype(jnp.float32)
            d_i.append((near - away) * sign)
            edge = jnp.zeros((ROWS, 128), jnp.float32)
            d_j.append(
                jnp.concatenate([here[:, 128:], edge], axis=1)
                - jnp.concatenate([edge, here[:, :-128]], axis=1)
            )
            d_k.append(
                jnp.where(lane == 127, 0.0, pltpu.roll(here, cells - 1, 1))
                - jnp.where(lane == 0, 0.0, pltpu.roll(here, 1, 1))
            )

        def deriv(comp, a):
            return (
                coef_ref[pl.ds(3 * a, 1), :] * d_i[comp]
                + coef_ref[pl.ds(3 * a + 1, 1), :] * d_j[comp]
                + coef_ref[pl.ds(3 * a + 2, 1), :] * d_k[comp]
            )

        for c, (p, q) in enumerate(((2, 1), (0, 2), (1, 0))):
            gathered[s, rows(t), part(c)] = (
                deriv(p, q) - deriv(q, p)
            ).astype(jnp.bfloat16)

    def launch(t, carry):
        for p in range(3):
            x_copy(t, p).start()
        return carry

    lax.fori_loop(0, chunks, launch, 0)

    rounds = n_space // 4 - 1
    signal(ring.at[0, 0], space=ahead)
    signal(ring.at[0, 1], space=behind)
    mask_copy.wait()
    for j in range(cells // 128):
        line = pl.ds(j, 1)
        weight = 0.5 * jnp.sqrt(volume_ref[line, :] * flags[0, j].astype(jnp.float32))
        coef_ref[:, pl.ds(j * 128, 128)] = metric_ref[:, j, :] * weight

    def step(t, carry):
        def forward(parts):
            @pl.when(t < chunks)
            def _():
                for p in parts:
                    x_copy(t, p).wait_recv()
                    z_copy(t, p).start()

        forward(range(2))

        @pl.when(jnp.logical_and(t >= Z_LAG, t < chunks + Z_LAG))
        def _():
            for p in range(3):
                z_copy(t - Z_LAG, p).wait_recv()
            vorticity(t - Z_LAG)
            for p in range(3):
                for o in range(1, chips):
                    y_copy(o, t - Z_LAG, p).start()
            m_copy(t - Z_LAG).start()

        forward(range(2, 3))

        @pl.when(t >= Y_LAG)
        def _():
            for p in range(3):
                for o in range(1, chips):
                    y_arrival(o, t - Y_LAG, p).wait_recv()
                    f_copy(o, t - Y_LAG, p).start()

        return carry

    def r_copy(block):
        return remote(
            partial.at[block], landed.at[i], r_s.at[block], r_r.at[i], space=block
        )

    def r_arrival(source):
        return remote(
            partial.at[i], landed.at[source], r_s.at[source], r_r.at[source], space=source
        )

    def product(dev, h):
        block = dev * per_dev + h
        partial[block] = lax.dot_general(
            gathered[dev, pl.ds(h * cols, cols), :], gathered[s], (((1,), (1,)), ((), ())),
            preferred_element_type=jnp.float32,
        )

        @pl.when(block != i)
        def _():
            r_copy(block).start()

    def await_m(t, carry):
        m_arrival(t).wait_recv()
        return carry

    per_block = cols // ROWS

    def product_f(o, h):
        def await_f(t, carry):
            for p in range(3):
                f_arrival(o, t, p).wait_recv()
            return carry

        lax.fori_loop(h * per_block, (h + 1) * per_block, await_f, 0)
        product(f_origin(o), h)

    def whole_product(dev):
        result = lax.dot_general(
            gathered[dev], gathered[s], (((1,), (1,)), ((), ())),
            preferred_element_type=jnp.float32,
        )
        for h in range(per_dev):
            block = dev * per_dev + h
            partial[block] = result[h * cols:(h + 1) * cols]

            @pl.when(block != i)
            def _():
                r_copy(block).start()

    done = chunks + Z_LAG
    lax.fori_loop(0, chunks // 2, step, 0)
    for n in range(rounds):
        pl.semaphore_wait(ring.at[n, 0], 1)
        pl.semaphore_wait(ring.at[n, 1], 1)
        if n < rounds - 1:
            signal(ring.at[n + 1, 0], space=ahead)
            signal(ring.at[n + 1, 1], space=behind)
    signal(pair, space=partner)
    lax.fori_loop(chunks // 2, done, step, 0)
    pl.semaphore_wait(pair, 1)
    whole_product(s)
    lax.fori_loop(0, chunks, await_m, 0)
    whole_product(mate)
    lax.fori_loop(done, chunks + Y_LAG - 1, step, 0)
    for o in range(1, chips):
        for h in range(per_dev - 1):
            product(origin(o), h)
    for o in range(1, chips):
        for h in range(per_dev - 1):
            product_f(o, h)
    lax.fori_loop(chunks + Y_LAG - 1, chunks + Y_LAG, step, 0)
    for o in range(1, chips):
        product(origin(o), per_dev - 1)
    for o in range(1, chips):
        product_f(o, per_dev - 1)

    def add(d, total):
        source = lax.rem(i + d, n_space)
        r_arrival(source).wait_recv()
        return total + landed[source]

    total = lax.fori_loop(1, n_space, add, partial[i])
    out_ref[...] = total

    def drain(t, carry):
        m_copy(t).wait_send()
        for p in range(3):
            x_copy(t, p).wait_send()
            z_copy(t, p).wait_send()
            for o in range(1, chips):
                y_copy(o, t, p).wait_send()
                f_copy(o, t, p).wait_send()
        return carry

    lax.fori_loop(0, chunks, drain, 0)

    def drain_r(d, carry):
        r_copy(lax.rem(i + d, n_space)).wait_send()
        return carry

    lax.fori_loop(1, n_space, drain_r, 0)


def shards(n_space, n_snap, velocity, metric, volume, blade_mask):
    snaps = velocity.shape[0]
    u = velocity.reshape(snaps, -1)
    width = u.shape[1]
    cols = snaps * n_snap // n_space
    chunks = snaps // ROWS
    chips = n_snap // 2
    far = max(chips - 1, 1)
    dma = pltpu.SemaphoreType.DMA
    return pl.pallas_call(
        functools.partial(kernel, n_space, n_snap),
        out_shape=jax.ShapeDtypeStruct((cols, snaps), jnp.float32),
        in_specs=[pl.BlockSpec(memory_space=pltpu.VMEM)] * 3
        + [pl.BlockSpec(memory_space=pltpu.HBM)],
        out_specs=pl.BlockSpec(memory_space=pltpu.VMEM),
        scratch_shapes=[
            pltpu.VMEM((9, width // 3), jnp.float32),
            pltpu.VMEM((snaps, width), jnp.bfloat16),
            pltpu.VMEM((snaps, width), jnp.bfloat16),
            pltpu.VMEM((n_snap, snaps, width), jnp.bfloat16),
            pltpu.VMEM((n_space, cols, snaps), jnp.float32),
            pltpu.VMEM((n_space, cols, snaps), jnp.float32),
            dma((chunks, 3)), dma((chunks, 3)), dma((chunks, 3)), dma((chunks, 3)),
            dma((chunks,)), dma((chunks,)),
            dma((far, chunks, 3)), dma((far, chunks, 3)),
            dma((far, chunks, 3)), dma((far, chunks, 3)),
            dma((n_space,)), dma((n_space,)),
            pltpu.SMEM(blade_mask.shape, jnp.int32), dma,
            pltpu.SemaphoreType.REGULAR((n_space // 4 - 1, 2)), pltpu.SemaphoreType.REGULAR,
        ],
        compiler_params=pltpu.CompilerParams(
            collective_id=0, has_side_effects=True, vmem_limit_bytes=48 * 1024 * 1024
        ),
    )(u, metric[:, 0], volume[0], blade_mask).T


def solution(mesh):
    in_specs = (
        P("snap", None, "space", None, None),
        P(None, "space", None, None),
        P("space", None, None),
        P("space", None),
    )
    body = functools.partial(shards, mesh.shape["space"], mesh.shape["snap"])
    return jax.shard_map(body, mesh=mesh, in_specs=in_specs, out_specs=P("snap", "space"), check_vma=False)
```
